32 devices in a mesh: ctx: 8 (over z, y), fsdp: 4 (over x, core).
Axes of the slice: x: 2, y: 2, z: 4, core: 2. Of those that a mesh axis runs over, the one named last changes fastest.
Arguments:
- inputs: bfloat16 [4, 4096, 2048], P('fsdp', 'ctx'), may hold values from -6 to 6
- queries: bfloat16 [4, 4096, 512], P('fsdp', 'ctx'), may hold values from -5 to 5
- key_vectors: bfloat16 [4, 4096, 128], P('fsdp', 'ctx'), may hold values from -5 to 5
- w_value: bfloat16 [2048, 128], P('fsdp'), may hold values from -0.125 to 0.125
- grad_out: bfloat16 [4, 4096, 512], P('fsdp', 'ctx'), may hold values from -6 to 6
- block_picks: int32 [4, 8, 2], P('fsdp'), may hold values from 0 to 6, as said below
Outputs:
- grad_queries: bfloat16 [4, 4096, 512], P('fsdp', 'ctx')
- grad_keys: bfloat16 [4, 4096, 128], P('fsdp', 'ctx')
- grad_values: bfloat16 [4, 4096, 128], P('fsdp', 'ctx')
- grad_weight: bfloat16 [2048, 128], P(('ctx', 'fsdp'))
The draws below stay inside these ranges and needn't reach their ends.
Inputs may be any that keep to these rules, and one draw needn't show every extreme that they name: `block_picks`: for query block b of a sequence the two entries are block indices no greater than b: for b >= 2 two different blocks below b, for b = 1 the pair 0 and 1, for b = 0 both 0. The last query block of every sequence selects block 6 as its second entry.
All inputs are finite; a program needn't handle non-finite values.
Results may differ from the reference program's by a relative error of at most 0.015.
Values may be sent and summed in bfloat16 or wider, within the bound.
A program may use at most 64 MiB of HBM per device.

```python
import functools
import math
import jax
import jax.numpy as jnp
from jax import lax

D = 2048
HEAD = 128
GROUP = 4
BLOCK = 512
TOK_DEV = 512
LENGTH = 4096
BLOCKS = 8
SEQUENCES = 4
N_CTX = 8


def drawn_pair(key):
    base = jax.random.fold_in(key, 7)
    key_query, key_keys = jax.random.split(base, 2)
    shape_query = (SEQUENCES, LENGTH, GROUP, HEAD)
    shape_keys = (SEQUENCES, LENGTH, HEAD)
    query_drawn = jnp.clip(jax.random.normal(key_query, shape_query, jnp.float32), -4.0, 4.0)
    keys_drawn = jnp.clip(jax.random.normal(key_keys, shape_keys, jnp.float32), -4.0, 4.0)
    return (query_drawn.reshape(SEQUENCES, LENGTH, GROUP * HEAD), keys_drawn)


def draw_queries(key, part):
    return drawn_pair(key)[0].astype(jnp.bfloat16)


def draw_key_vectors(key, part):
    return drawn_pair(key)[1].astype(jnp.bfloat16)


def draw_block_picks(key, part):
    base = jax.random.fold_in(key, 23)
    key_first, key_second = jax.random.split(base)
    block_id = jnp.arange(BLOCKS, dtype=jnp.int32)[None, :]
    span = jnp.maximum(block_id, 1)
    first_pick = jax.random.randint(key_first, (SEQUENCES, BLOCKS), 0, span)
    step_size = jax.random.randint(key_second, (SEQUENCES, BLOCKS), 0, jnp.maximum(block_id - 1, 1))
    second_pick = (first_pick + 1 + step_size) % span
    last_block = block_id == BLOCKS - 1
    first_pick = jnp.where(last_block, first_pick % (BLOCKS - 2), first_pick)
    second_pick = jnp.where(last_block, BLOCKS - 2, second_pick)
    second_pick = jnp.where(block_id == 1, 1, second_pick)
    first_pick = jnp.where(block_id == 0, 0, first_pick)
    second_pick = jnp.where(block_id == 0, 0, second_pick)
    return jnp.stack([first_pick, second_pick], axis=2).astype(jnp.int32)


def spiked(values, rng, source, target, parts, factor):
    def block_of(dim):
        return (jnp.arange(values.shape[dim]) // (values.shape[dim] // parts)).reshape((-1,) + (1,) * (values.ndim - 1 - dim))

    near = jax.random.permutation(rng, parts)[block_of(target)]
    far = (block_of(target) + parts // 2) % parts
    return jnp.where((block_of(source) == near) | (block_of(source) == far), factor * values, values)


def block_scale(rng, shape, cuts, smallest, largest):
    gain = 1.0
    for axis_at, parts in cuts:
        steps = jax.random.uniform(jax.random.fold_in(jax.random.fold_in(rng, 6), axis_at), (parts,), jnp.float32, smallest / len(cuts), largest / len(cuts))
        gain = gain * jnp.repeat(jnp.exp(steps), shape[axis_at] // parts).reshape((-1,) + (1,) * (len(shape) - 1 - axis_at))
    return gain


def noise(stream_key, shape, spread, reach, pieces=(), held_as=jnp.bfloat16):
    loudness = block_scale(stream_key, shape, pieces, -0.22, 0.18) if pieces else 1.0
    result = jax.random.normal(stream_key, shape, jnp.float32) * spread * loudness
    return jnp.minimum(jnp.maximum(result, -reach), reach).astype(held_as)


def heavy_noise(own_key, extent, deviation, limit, shards, heavy, kind=jnp.bfloat16):
    values = deviation * jax.random.normal(own_key, extent, jnp.float32)
    if shards:
        values = values * block_scale(own_key, extent, shards, -0.22, 0.18)
    return jnp.clip(spiked(values, jax.random.fold_in(own_key, 3), *heavy), -limit, limit).astype(kind)


def setup_inputs(seed: int = 0) -> dict:
    keys = jax.random.split(jax.random.key(seed), 7)
    inputs = heavy_noise(keys[0], (SEQUENCES, LENGTH, D), 1.0, 6.0, ((0, 4), (1, 8)), (1, 2, 8, 2.0))
    queries = draw_queries(jax.random.fold_in(keys[6], 71), 0)
    key_vectors = draw_key_vectors(jax.random.fold_in(keys[6], 71), 0)
    w_value = noise(keys[3], (D, HEAD), D ** -0.5, 0.125, ((0, 4),))
    grad_out = noise(keys[4], (SEQUENCES, LENGTH, GROUP * HEAD), 1.0, 6.0, ((0, 4), (1, 8)))
    block_picks = draw_block_picks(jax.random.fold_in(keys[6], 71), 0)
    return dict(inputs=inputs, queries=queries, key_vectors=key_vectors, w_value=w_value, grad_out=grad_out, block_picks=block_picks)


NEG = -1e+30

def block_pass(query_rows, grad_rows, key_all, value_all, chosen, block_id):
    inv_root = 1.0 / math.sqrt(HEAD)
    key_block = jnp.concatenate([lax.dynamic_slice_in_dim(key_all, (chosen[slot_index] * BLOCK).astype(jnp.int32), BLOCK, 0) for slot_index in range(3)], axis=0).astype(jnp.float32)
    value_block = jnp.concatenate([lax.dynamic_slice_in_dim(value_all, (chosen[slot_index] * BLOCK).astype(jnp.int32), BLOCK, 0) for slot_index in range(3)], axis=0).astype(jnp.float32)
    query_heads = query_rows.reshape(BLOCK, GROUP, HEAD).astype(jnp.float32)
    grad_heads = grad_rows.reshape(BLOCK, GROUP, HEAD).astype(jnp.float32)
    query_pos = block_id * BLOCK + jnp.arange(BLOCK, dtype=jnp.int32)
    key_pos = (chosen[:, None] * BLOCK + jnp.arange(BLOCK, dtype=jnp.int32)[None, :]).reshape(-1)
    slot_of = jnp.repeat(jnp.arange(3, dtype=jnp.int32), BLOCK)
    usable = chosen != block_id
    allowed = jnp.where(slot_of[None, :] == 0, key_pos[None, :] <= query_pos[:, None], usable[slot_of][None, :])
    scores = jnp.einsum('tgh,uh->gtu', query_heads, key_block) * inv_root
    masked = jnp.where(allowed[None], scores, NEG)
    highest = lax.optimization_barrier(jnp.max(masked, axis=2, keepdims=True))
    exp_terms = jnp.where(allowed[None], jnp.exp(masked - highest), 0.0)
    weights = exp_terms / lax.optimization_barrier(jnp.sum(exp_terms, axis=2, keepdims=True))
    weights_low = weights.astype(jnp.bfloat16).astype(jnp.float32)
    attended = jnp.einsum('gtu,uh->tgh', weights_low, value_block)
    row_delta = lax.optimization_barrier(jnp.sum(grad_heads * attended, axis=2))
    dweights = jnp.einsum('tgh,uh->gtu', grad_heads, value_block)
    dscores = (weights * (dweights - row_delta.T[:, :, None])).astype(jnp.bfloat16).astype(jnp.float32)
    grad_query_rows = (jnp.einsum('gtu,uh->tgh', dscores, key_block) * inv_root).astype(jnp.bfloat16)
    key_part = jnp.einsum('gtu,tgh->uh', dscores, query_heads) * inv_root
    value_part = jnp.einsum('gtu,tgh->uh', weights_low, grad_heads)
    partial_kv = jnp.concatenate([key_part, value_part], axis=1)
    return (grad_query_rows.reshape(BLOCK, GROUP * HEAD), partial_kv)

def sequence_pass(w_value, arrays):
    source, query_all, key_all, grad_all, pick_table = arrays
    projected = jnp.dot(source, w_value, preferred_element_type=jnp.float32).astype(jnp.bfloat16)
    local_count = TOK_DEV // BLOCK

    def step_shard(running, shard_id):
        buffer = jnp.zeros((LENGTH, 2 * HEAD), jnp.float32)
        grad_pieces = []
        for local_index in range(local_count):
            block_id = (shard_id * local_count + local_index).astype(jnp.int32)
            picked = lax.dynamic_index_in_dim(pick_table, block_id, 0, keepdims=False)
            chosen = jnp.concatenate([block_id[None], picked]).astype(jnp.int32)
            query_rows = lax.dynamic_slice_in_dim(query_all, (block_id * BLOCK).astype(jnp.int32), BLOCK, 0)
            grad_rows = lax.dynamic_slice_in_dim(grad_all, (block_id * BLOCK).astype(jnp.int32), BLOCK, 0)
            grad_query_rows, partial_kv = block_pass(query_rows, grad_rows, key_all, projected, chosen, block_id)
            slots = partial_kv.reshape(3, BLOCK, 2 * HEAD)
            for slot_index in range(3):
                begin_row = (chosen[slot_index] * BLOCK).astype(jnp.int32)
                current = lax.dynamic_slice_in_dim(buffer, begin_row, BLOCK, 0)
                buffer = lax.dynamic_update_slice_in_dim(buffer, current + slots[slot_index], begin_row, 0)
            grad_pieces.append(grad_query_rows)
        rounded = lax.optimization_barrier(buffer.astype(jnp.bfloat16))
        return (running + rounded.astype(jnp.float32), jnp.concatenate(grad_pieces, axis=0))
    running, grad_blocks = lax.scan(step_shard, jnp.zeros((LENGTH, 2 * HEAD), jnp.float32), jnp.arange(N_CTX, dtype=jnp.int32))
    grad_query_all = grad_blocks.reshape(LENGTH, GROUP * HEAD)
    grad_key_all = running[:, :HEAD].astype(jnp.bfloat16)
    grad_value_all = running[:, HEAD:].astype(jnp.bfloat16)
    weight_part = jnp.dot(source.T, grad_value_all, preferred_element_type=jnp.float32)
    return (grad_query_all, grad_key_all, grad_value_all, weight_part)

def reference(inputs, queries, key_vectors, w_value, grad_out, block_picks):
    results = lax.map(functools.partial(sequence_pass, w_value), (inputs, queries, key_vectors, grad_out, block_picks))
    grad_weight = lax.optimization_barrier(jnp.sum(results[3], axis=0)).astype(jnp.bfloat16)
    return (results[0], results[1], results[2], grad_weight)
```

```python
import math

import jax
import jax.numpy as jnp
from jax import lax
from jax.experimental import pallas as pl
from jax.experimental.pallas import tpu as pltpu
from jax.sharding import PartitionSpec as P

HEAD = 128
GROUP = 4
BLOCK = 512
NEG = -1e30
MESH = pl.DeviceIdType.MESH
F32 = jnp.float32
BF16 = jnp.bfloat16
VM = pltpu.VMEM


def bits_of(count):
    bits, bit = [], 1
    while bit < count:
        bits.append(bit)
        bit *= 2
    return bits


def remote(src, dst, send, recv, **where):
    return pltpu.make_async_remote_copy(
        src_ref=src,
        dst_ref=dst,
        send_sem=send,
        recv_sem=recv,
        device_id=where,
        device_id_type=MESH,
    )


def greet(n, nf, direct):
    c, f = lax.axis_index("ctx"), lax.axis_index("fsdp")
    lines = n // 2
    y, z = c % 2, c // 2
    barrier = pltpu.get_barrier_semaphore()
    count = 0
    for bit in bits_of(nf):
        mine = (f // bit) % 2
        pl.semaphore_signal(
            barrier, inc=1, device_id={"fsdp": f + bit - 2 * bit * mine}, device_id_type=MESH
        )
        count += 1
    pl.semaphore_signal(
        barrier, inc=1, device_id={"ctx": 2 * z + (1 - y)}, device_id_type=MESH
    )
    count += 1
    if direct:
        for o in range(1, lines):
            pl.semaphore_signal(
                barrier, inc=1, device_id={"ctx": 2 * ((z + o) % lines) + y}, device_id_type=MESH
            )
            count += 1
        pl.semaphore_wait(barrier, count)
    else:
        pl.semaphore_wait(barrier, count)

        @pl.when(z > 0)
        def _():
            pl.semaphore_signal(barrier, inc=1, device_id={"ctx": c - 2}, device_id_type=MESH)

        @pl.when(z < lines - 1)
        def _():
            pl.semaphore_signal(barrier, inc=1, device_id={"ctx": c + 2}, device_id_type=MESH)

        @pl.when(z > 0)
        def _():
            pl.semaphore_wait(barrier, 1)

        @pl.when(z < lines - 1)
        def _():
            pl.semaphore_wait(barrier, 1)


def gather_kernel(
    n, nf, x_ref, k_ref, w_ref, kall, vall, wbuf, w_send, w_recv,
    kz_send, vz_send, ky_send, vy_send, k_recv, v_recv,
):
    c, f = lax.axis_index("ctx"), lax.axis_index("fsdp")
    lines = n // 2
    y, z = c % 2, c // 2
    partner = 2 * z + (1 - y)
    ws = w_ref.shape[0]
    wbuf[f] = w_ref[...]
    kall[c] = k_ref[...]
    greet(n, nf, True)

    def up(buf, b, send, recv):
        return remote(buf.at[b], buf.at[b], send.at[b], recv.at[b], ctx=c + 2)

    def across(buf, b, send, recv):
        return remote(buf.at[b], buf.at[b], send.at[b], recv.at[b], ctx=partner)

    held = [f]
    bits = bits_of(nf)
    slot = 0
    stages = []
    for bit in reversed(bits):
        mine = (f // bit) % 2
        other = bit - 2 * bit * mine
        stages.append((bit, other))

    def w_stage(index, held, slot):
        bit, other = stages[index]
        copies = []
        for g in held:
            copies.append(
                remote(wbuf.at[g], wbuf.at[g], w_send.at[slot], w_recv.at[slot], fsdp=f + other)
            )
            slot += 1
        for copy in copies:
            copy.start()
        return copies, [g + other for g in held], slot

    def forward(buf, b, zsend, ysend, recv, first):
        @pl.when(z < lines - 1)
        def _():
            up(buf, b, zsend, recv).start()

        if first:
            @pl.when(y == 0)
            def _():
                across(buf, b, ysend, recv).start()
        else:
            across(buf, b, ysend, recv).start()

    total = None

    def add(total, g):
        columns = pl.ds(pl.multiple_of(g * ws, ws), ws)
        term = jnp.dot(x_ref[:, columns], wbuf[g], preferred_element_type=F32)
        return term if total is None else total + term

    for index in range(len(stages)):
        copies, came, slot = w_stage(index, held, slot)
        if index == 0:
            forward(kall, c, kz_send, ky_send, k_recv, True)
            total = add(total, f)
        for copy in copies:
            copy.wait()
        held = held + came
    for g in held[1:]:
        total = add(total, g)
    vall[c] = total.astype(BF16)
    forward(vall, c, vz_send, vy_send, v_recv, True)

    for s in range(1, lines):
        b = c - 2 * s

        @pl.when(z - s >= 0)
        def _():
            up(kall, b, kz_send, k_recv).wait_recv()
            forward(kall, b, kz_send, ky_send, k_recv, False)
            up(vall, b, vz_send, v_recv).wait_recv()
            forward(vall, b, vz_send, vy_send, v_recv, False)

    @pl.when(y == 1)
    def _():
        across(kall, partner, ky_send, k_recv).wait_recv()
        across(vall, partner, vy_send, v_recv).wait_recv()

    for s in range(1, lines):
        @pl.when(z - s >= 0)
        def _():
            across(kall, partner - 2 * s, ky_send, k_recv).wait_recv()
            across(vall, partner - 2 * s, vy_send, v_recv).wait_recv()

    for s in range(lines):
        b = c - 2 * s

        @pl.when(z - s >= 0)
        def _():
            @pl.when(z < lines - 1)
            def _():
                up(kall, b, kz_send, k_recv).wait_send()
                up(vall, b, vz_send, v_recv).wait_send()

            def done():
                across(kall, b, ky_send, k_recv).wait_send()
                across(vall, b, vy_send, v_recv).wait_send()

            if s == 0:
                pl.when(y == 0)(done)
            else:
                done()


def attend_kernel(
    ids, q_ref, g_ref, k0, k1, k2, v0, v1, v2, dq_ref, own_k, own_v, slot_k, slot_v, dk_acc, dv_acc
):
    h = pl.program_id(0)
    inv_root = 1.0 / math.sqrt(HEAD)
    q = q_ref[...]
    g = g_ref[...]
    ks = [k0[...], k1[0], k2[0]]
    vs = [v0[0], v1[0], v2[0]]
    nt = (((1,), (1,)), ((), ()))
    tn = (((0,), (0,)), ((), ()))
    scores = []
    for j in range(3):
        s = lax.dot_general(ks[j], q, nt, preferred_element_type=F32) * inv_root
        if j == 0:
            u = lax.broadcasted_iota(jnp.int32, s.shape, 0)
            t = lax.broadcasted_iota(jnp.int32, s.shape, 1)
            s = jnp.where(u <= t, s, NEG)
        else:
            s = jnp.where(ids[j] != ids[0], s, NEG)
        scores.append(s)
    highest = jnp.max(
        jnp.maximum(jnp.maximum(scores[0], scores[1]), scores[2]), axis=0, keepdims=True
    )
    exps = [jnp.exp(s - highest) for s in scores]
    norm = 1.0 / jnp.sum(exps[0] + exps[1] + exps[2], axis=0, keepdims=True)
    weights = [e * norm for e in exps]
    lows = [w.astype(BF16) for w in weights]
    dws = [lax.dot_general(v, g, nt, preferred_element_type=F32) for v in vs]
    delta = jnp.sum(
        sum(low.astype(F32) * dw for low, dw in zip(lows, dws)), axis=0, keepdims=True
    )
    ds = [(w * (dw - delta)).astype(BF16) for w, dw in zip(weights, dws)]
    dq = sum(lax.dot_general(d, k, tn, preferred_element_type=F32) for d, k in zip(ds, ks))
    dq_ref[...] = (dq * inv_root).astype(BF16)

    @pl.when(h == 0)
    def _():
        dk_acc[...] = jnp.zeros_like(dk_acc)
        dv_acc[...] = jnp.zeros_like(dv_acc)

    for j in range(3):
        dk_acc[j] += jnp.dot(ds[j], q, preferred_element_type=F32)
        dv_acc[j] += jnp.dot(lows[j], g, preferred_element_type=F32)

    @pl.when(h == GROUP - 1)
    def _():
        own_k[...] = dk_acc[0] * inv_root
        own_v[...] = dv_acc[0]
        for j in (1, 2):
            slot_k[j - 1] = (dk_acc[j] * inv_root).astype(BF16)
            slot_v[j - 1] = dv_acc[j].astype(BF16)


def reduce_kernel(
    n, nf, picks, x_ref, own_k, own_v, slot_k, slot_v, gk_ref, gv_ref, gw_ref,
    pslot_k, pslot_v, sbuf_k, sbuf_v, rbuf_k, rbuf_v, acc, wsend, wrecv, ysend_buf, yrecv_buf,
    zsend_buf, zrecv_buf, p_send, p_recv, c_send, c_recv, f_send, f_recv, y_sem, z_send, z_recv,
):
    c, f = lax.axis_index("ctx"), lax.axis_index("fsdp")
    lines = n // 2
    y, z = c % 2, c // 2
    partner = 2 * z + (1 - y)
    greet(n, nf, True)
    sides = []
    for side, (slots, pslots) in enumerate(((slot_v, pslot_v), (slot_k, pslot_k))):
        copy = remote(slots, pslots, p_send.at[side], p_recv.at[side], ctx=partner)
        copy.start()
        sides.append(copy)

    def chain(side):
        own, slots, pslots, sbuf, rbuf, out = (
            (own_v, slot_v, pslot_v, sbuf_v, rbuf_v, gv_ref),
            (own_k, slot_k, pslot_k, sbuf_k, rbuf_k, gk_ref),
        )[side]

        def down(zd):
            return remote(
                sbuf.at[zd], rbuf.at[zd], c_send.at[side, zd], c_recv.at[side, zd], ctx=c - 2
            )

        sides[side].wait()
        for zd in range(lines):
            @pl.when(zd <= z)
            def _():
                dest = 2 * zd + y
                value = jnp.zeros(own.shape, F32)
                for owner, held in ((c, slots), (partner, pslots)):
                    for j in range(2):
                        gate = jnp.where(picks[owner, j] == dest, 1.0, 0.0).astype(F32)
                        value = value + held[j].astype(F32) * gate
                sbuf[zd] = value.astype(BF16)

                @pl.when(z < lines - 1)
                def _():
                    down(zd).wait_recv()
                    sbuf[zd] = (value + rbuf[zd].astype(F32)).astype(BF16)

                @pl.when(zd < z)
                def _():
                    down(zd).start()

                @pl.when(zd == z)
                def _():
                    out[...] = (sbuf[zd].astype(F32) + own[...]).astype(BF16)

        return down

    down_v = chain(0)
    gv = gv_ref[...]
    rows = x_ref.shape[1] // (n * nf)
    group = x_ref.shape[1] // n
    tn = (((0,), (0,)), ((), ()))
    part = lax.dot_general(x_ref[...], gv, tn, preferred_element_type=F32)
    for cc in range(n):
        for ff in range(nf):
            at = cc * group + ff * rows
            acc[ff, cc] = part[at : at + rows]

    slot = 0
    copies = []
    for stage, bit in enumerate(bits_of(nf)):
        mine = (f // bit) % 2
        low = f % bit
        now = []
        for hi in range(nf // (2 * bit)):
            away = hi * 2 * bit + (1 - mine) * bit + low
            wsend[slot] = acc[away].astype(BF16)
            copy = remote(
                wsend.at[slot], wrecv.at[slot], f_send.at[slot], f_recv.at[slot],
                fsdp=f + bit - 2 * bit * mine,
            )
            copy.start()
            now.append((copy, hi * 2 * bit + mine * bit + low, slot))
            slot += 1
        for copy, keep, at in now:
            copy.wait()
            acc[keep] += wrecv[at].astype(F32)
    for zz in range(lines):
        ysend_buf[zz] = acc[f, 2 * zz + (1 - y)].astype(BF16)
    copy = remote(ysend_buf, yrecv_buf, y_sem.at[0], y_sem.at[1], ctx=partner)
    copy.start()
    copy.wait()
    now = []
    for o in range(1, lines):
        zz = (z + o) % lines
        zsend_buf[o] = (acc[f, 2 * zz + y] + yrecv_buf[zz].astype(F32)).astype(BF16)
        copy = remote(
            zsend_buf.at[o], zrecv_buf.at[o], z_send.at[o], z_recv.at[o], ctx=2 * zz + y
        )
        copy.start()
        now.append(copy)
    total = acc[f, c] + yrecv_buf[z].astype(F32)
    for o, copy in enumerate(now):
        copy.wait()
        total = total + zrecv_buf[o + 1].astype(F32)
    gw_ref[...] = total.astype(BF16)

    down_k = chain(1)
    for zd in range(lines):
        @pl.when(zd < z)
        def _():
            down_v(zd).wait_send()
            down_k(zd).wait_send()


def on_device(inputs, queries, key_vectors, w_value, grad_out, block_picks):
    n, nf = lax.axis_size("ctx"), lax.axis_size("fsdp")
    c = lax.axis_index("ctx")
    lines = n // 2
    x, q, k, g, picks = inputs[0], queries[0], key_vectors[0], grad_out[0], block_picks[0]
    dma = pltpu.SemaphoreType.DMA
    vmem = pl.BlockSpec(memory_space=VM)
    smem = pl.BlockSpec(memory_space=pltpu.SMEM)
    ws = w_value.shape[0]
    kall, vall = pl.pallas_call(
        lambda *refs: gather_kernel(n, nf, *refs),
        out_shape=[jax.ShapeDtypeStruct((n, BLOCK, HEAD), BF16)] * 2,
        in_specs=[vmem] * 3,
        out_specs=[vmem] * 2,
        scratch_shapes=[VM((nf, ws, HEAD), BF16), dma((nf,)), dma((nf,))] + [dma((n,))] * 6,
        compiler_params=pltpu.CompilerParams(
            collective_id=0, has_side_effects=True, vmem_limit_bytes=48 * 2**20
        ),
        name="gather_kv",
    )(x, k, w_value)

    ids = jnp.concatenate([c[None].astype(jnp.int32), lax.dynamic_index_in_dim(picks, c, 0, False)])
    block = (1, BLOCK, HEAD)
    head = pl.BlockSpec((BLOCK, HEAD), lambda h, ids: (0, h))
    fixed2 = pl.BlockSpec((BLOCK, HEAD), lambda h, ids: (0, 0))
    pair = pl.BlockSpec((2, BLOCK, HEAD), lambda h, ids: (0, 0, 0))
    at = [pl.BlockSpec(block, lambda h, ids, j=j: (ids[j], 0, 0)) for j in range(3)]
    dq, own_k, own_v, slot_k, slot_v = pl.pallas_call(
        attend_kernel,
        out_shape=[
            jax.ShapeDtypeStruct((BLOCK, GROUP * HEAD), BF16),
            jax.ShapeDtypeStruct((BLOCK, HEAD), F32),
            jax.ShapeDtypeStruct((BLOCK, HEAD), F32),
            jax.ShapeDtypeStruct((2, BLOCK, HEAD), BF16),
            jax.ShapeDtypeStruct((2, BLOCK, HEAD), BF16),
        ],
        grid_spec=pltpu.PrefetchScalarGridSpec(
            num_scalar_prefetch=1,
            grid=(GROUP,),
            in_specs=[head, head, fixed2, at[1], at[2], at[0], at[1], at[2]],
            out_specs=[head, fixed2, fixed2, pair, pair],
            scratch_shapes=[VM((3, BLOCK, HEAD), F32)] * 2,
        ),
        compiler_params=pltpu.CompilerParams(vmem_limit_bytes=48 * 2**20),
        name="attend",
    )(ids, q, g, k, kall, kall, vall, vall, vall)

    rows = x.shape[1] // (n * nf)
    line_buf = VM((lines, BLOCK, HEAD), BF16)
    gk, gv, gw = pl.pallas_call(
        lambda *refs: reduce_kernel(n, nf, *refs),
        out_shape=[
            jax.ShapeDtypeStruct((BLOCK, HEAD), BF16),
            jax.ShapeDtypeStruct((BLOCK, HEAD), BF16),
            jax.ShapeDtypeStruct((rows, HEAD), BF16),
        ],
        in_specs=[smem] + [vmem] * 5,
        out_specs=[vmem] * 3,
        scratch_shapes=[VM((2, BLOCK, HEAD), BF16)] * 2
        + [line_buf] * 4
        + [
            VM((nf, n, rows, HEAD), F32),
            VM((nf, n, rows, HEAD), BF16),
            VM((nf, n, rows, HEAD), BF16),
        ]
        + [VM((lines, rows, HEAD), BF16)] * 4
        + [
            dma((2,)), dma((2,)), dma((2, lines)), dma((2, lines)), dma((nf,)), dma((nf,)),
            dma((2,)), dma((lines,)), dma((lines,)),
        ],
        compiler_params=pltpu.CompilerParams(
            collective_id=1, has_side_effects=True, vmem_limit_bytes=56 * 2**20
        ),
        name="reduce_grads",
    )(picks, x, own_k, own_v, slot_k, slot_v)
    return dq[None], gk[None], gv[None], gw


def solution(mesh):
    in_specs = (
        P("fsdp", "ctx", None),
        P("fsdp", "ctx", None),
        P("fsdp", "ctx", None),
        P("fsdp", None),
        P("fsdp", "ctx", None),
        P("fsdp", None, None),
    )
    out_specs = (
        P("fsdp", "ctx", None),
        P("fsdp", "ctx", None),
        P("fsdp", "ctx", None),
        P(("ctx", "fsdp"), None),
    )
    return jax.shard_map(
        on_device, mesh=mesh, in_specs=in_specs, out_specs=out_specs, check_vma=False
    )
```

```python
import math

import jax
import jax.numpy as jnp
from jax import lax
from jax.experimental import pallas as pl
from jax.experimental.pallas import tpu as pltpu
from jax.sharding import PartitionSpec as P

HEAD = 128
GROUP = 4
BLOCK = 512
NEG = -1e30
MESH = pl.DeviceIdType.MESH
F32 = jnp.float32
BF16 = jnp.bfloat16
VM = pltpu.VMEM


def bits_of(count):
    bits, bit = [], 1
    while bit < count:
        bits.append(bit)
        bit *= 2
    return bits


def remote(src, dst, send, recv, **where):
    return pltpu.make_async_remote_copy(
        src_ref=src,
        dst_ref=dst,
        send_sem=send,
        recv_sem=recv,
        device_id=where,
        device_id_type=MESH,
    )


def greet(n, nf, direct):
    c, f = lax.axis_index("ctx"), lax.axis_index("fsdp")
    lines = n // 2
    y, z = c % 2, c // 2
    barrier = pltpu.get_barrier_semaphore()
    count = 0
    for bit in bits_of(nf):
        mine = (f // bit) % 2
        pl.semaphore_signal(
            barrier, inc=1, device_id={"fsdp": f + bit - 2 * bit * mine}, device_id_type=MESH
        )
        count += 1
    pl.semaphore_signal(
        barrier, inc=1, device_id={"ctx": 2 * z + (1 - y)}, device_id_type=MESH
    )
    count += 1
    if direct:
        for o in range(1, lines):
            pl.semaphore_signal(
                barrier, inc=1, device_id={"ctx": 2 * ((z + o) % lines) + y}, device_id_type=MESH
            )
            count += 1
        pl.semaphore_wait(barrier, count)
    else:
        pl.semaphore_wait(barrier, count)

        @pl.when(z > 0)
        def _():
            pl.semaphore_signal(barrier, inc=1, device_id={"ctx": c - 2}, device_id_type=MESH)

        @pl.when(z < lines - 1)
        def _():
            pl.semaphore_signal(barrier, inc=1, device_id={"ctx": c + 2}, device_id_type=MESH)

        @pl.when(z > 0)
        def _():
            pl.semaphore_wait(barrier, 1)

        @pl.when(z < lines - 1)
        def _():
            pl.semaphore_wait(barrier, 1)


def gather_kernel(
    n, nf, x_hbm, k_hbm, w_hbm, kall, vall, x_ref, wbuf, load, w_send, w_recv,
    kz_send, vz_send, ky_send, vy_send, k_recv, v_recv,
):
    c, f = lax.axis_index("ctx"), lax.axis_index("fsdp")
    lines = n // 2
    y, z = c % 2, c // 2
    partner = 2 * z + (1 - y)
    ws = w_hbm.shape[0]
    loads = [
        pltpu.make_async_copy(w_hbm, wbuf.at[f], load.at[0]),
        pltpu.make_async_copy(k_hbm, kall.at[c], load.at[1]),
        pltpu.make_async_copy(x_hbm, x_ref, load.at[2]),
    ]
    for copy in loads:
        copy.start()
    greet(n, nf, True)
    loads[0].wait()
    loads[1].wait()

    def up(buf, b, send, recv):
        return remote(buf.at[b], buf.at[b], send.at[b], recv.at[b], ctx=c + 2)

    def across(buf, b, send, recv):
        return remote(buf.at[b], buf.at[b], send.at[b], recv.at[b], ctx=partner)

    held = [f]
    bits = bits_of(nf)
    slot = 0
    stages = []
    for bit in reversed(bits):
        mine = (f // bit) % 2
        other = bit - 2 * bit * mine
        stages.append((bit, other))

    def w_stage(index, held, slot):
        bit, other = stages[index]
        copies = []
        for g in held:
            copies.append(
                remote(wbuf.at[g], wbuf.at[g], w_send.at[slot], w_recv.at[slot], fsdp=f + other)
            )
            slot += 1
        for copy in copies:
            copy.start()
        return copies, [g + other for g in held], slot

    def forward(buf, b, zsend, ysend, recv, first):
        @pl.when(z < lines - 1)
        def _():
            up(buf, b, zsend, recv).start()

        if first:
            @pl.when(y == 0)
            def _():
                across(buf, b, ysend, recv).start()
        else:
            across(buf, b, ysend, recv).start()

    total = None

    def add(total, g):
        columns = pl.ds(pl.multiple_of(g * ws, ws), ws)
        term = jnp.dot(x_ref[:, columns], wbuf[g], preferred_element_type=F32)
        return term if total is None else total + term

    def relay(buf, s, zsend, ysend, recv):
        b = c - 2 * s

        @pl.when(z - s >= 0)
        def _():
            up(buf, b, zsend, recv).wait_recv()
            forward(buf, b, zsend, ysend, recv, False)

    early = 1
    for index in range(len(stages)):
        copies, came, slot = w_stage(index, held, slot)
        if index == 0:
            forward(kall, c, kz_send, ky_send, k_recv, True)
            loads[2].wait()
            total = add(total, f)
            for s in range(1, 1 + early):
                relay(kall, s, kz_send, ky_send, k_recv)
        for copy in copies:
            copy.wait()
        held = held + came
    for g in held[1:]:
        total = add(total, g)
    vall[c] = total.astype(BF16)
    forward(vall, c, vz_send, vy_send, v_recv, True)

    for s in range(1, lines):
        if s + early < lines:
            relay(kall, s + early, kz_send, ky_send, k_recv)
        relay(vall, s, vz_send, vy_send, v_recv)

    @pl.when(y == 1)
    def _():
        across(kall, partner, ky_send, k_recv).wait_recv()
        across(vall, partner, vy_send, v_recv).wait_recv()

    for s in range(1, lines):
        @pl.when(z - s >= 0)
        def _():
            across(kall, partner - 2 * s, ky_send, k_recv).wait_recv()
            across(vall, partner - 2 * s, vy_send, v_recv).wait_recv()

    for s in range(lines):
        b = c - 2 * s

        @pl.when(z - s >= 0)
        def _():
            @pl.when(z < lines - 1)
            def _():
                up(kall, b, kz_send, k_recv).wait_send()
                up(vall, b, vz_send, v_recv).wait_send()

            def done():
                across(kall, b, ky_send, k_recv).wait_send()
                across(vall, b, vy_send, v_recv).wait_send()

            if s == 0:
                pl.when(y == 0)(done)
            else:
                done()


def attend_kernel(
    me, picks, q_ref, g_ref, k0, k1, k2, v0, v1, v2, dq_ref, own_k, own_v, slot_k, slot_v, dk_acc, dv_acc
):
    h = pl.program_id(0)
    inv_root = 1.0 / math.sqrt(HEAD)
    q = q_ref[...]
    g = g_ref[...]
    ks = [k0[...], k1[0], k2[0]]
    vs = [v0[0], v1[0], v2[0]]
    nt = (((1,), (1,)), ((), ()))
    tn = (((0,), (0,)), ((), ()))
    scale = inv_root / math.log(2.0)
    scores, tops = [], []
    for j in range(3):
        s = lax.dot_general(ks[j], q, nt, preferred_element_type=F32)
        if j == 0:
            u = lax.broadcasted_iota(jnp.int32, s.shape, 0)
            t = lax.broadcasted_iota(jnp.int32, s.shape, 1)
            s = jnp.where(u <= t, s, NEG)
        scores.append(s)
        tops.append(jnp.max(s, axis=0, keepdims=True))
    use = [picks[me[0], j] != me[0] for j in range(2)]
    highest = tops[0]
    for j in range(2):
        highest = jnp.maximum(highest, jnp.where(use[j], tops[j + 1], NEG))
    highest = highest * scale
    shifts = [highest] + [jnp.where(use[j], highest, -NEG) for j in range(2)]
    exps = [jnp.exp2(s * scale - shift) for s, shift in zip(scores, shifts)]
    norm = 1.0 / sum(jnp.sum(e, axis=0, keepdims=True) for e in exps)
    weights = [e * norm for e in exps]
    lows = [w.astype(BF16) for w in weights]
    dws = [lax.dot_general(v, g, nt, preferred_element_type=F32) for v in vs]
    delta = sum(
        jnp.sum(low.astype(F32) * dw, axis=0, keepdims=True) for low, dw in zip(lows, dws)
    )
    ds = [(w * (dw - delta)).astype(BF16) for w, dw in zip(weights, dws)]
    dq = sum(lax.dot_general(d, k, tn, preferred_element_type=F32) for d, k in zip(ds, ks))
    dq_ref[...] = (dq * inv_root).astype(BF16)

    @pl.when(h == 0)
    def _():
        dk_acc[...] = jnp.zeros_like(dk_acc)
        dv_acc[...] = jnp.zeros_like(dv_acc)

    for j in range(3):
        dk_acc[j] += jnp.dot(ds[j], q, preferred_element_type=F32)
        dv_acc[j] += jnp.dot(lows[j], g, preferred_element_type=F32)

    @pl.when(h == GROUP - 1)
    def _():
        own_k[...] = dk_acc[0] * inv_root
        own_v[...] = dv_acc[0]
        for j in (1, 2):
            slot_k[j - 1] = (dk_acc[j] * inv_root).astype(BF16)
            slot_v[j - 1] = dv_acc[j].astype(BF16)


def reduce_kernel(
    n, nf, picks, x_hbm, own_k, own_v, slot_k, slot_v, gk_ref, gv_ref, gw_ref,
    pslot_k, pslot_v, sbuf_k, sbuf_v, rbuf_k, rbuf_v, acc, wsend, wrecv, ysend_buf, yrecv_buf,
    zsend_buf, zrecv_buf, x_ref, xt, load, p_send, p_recv, c_send, c_recv, f_send, f_recv, y_sem, z_send, z_recv,
):
    c, f = lax.axis_index("ctx"), lax.axis_index("fsdp")
    lines = n // 2
    y, z = c % 2, c // 2
    partner = 2 * z + (1 - y)
    fetch = pltpu.make_async_copy(x_hbm, x_ref, load.at[0])
    fetch.start()
    greet(n, nf, True)
    sides = []
    for side, (slots, pslots) in enumerate(((slot_v, pslot_v), (slot_k, pslot_k))):
        copy = remote(slots, pslots, p_send.at[side], p_recv.at[side], ctx=partner)
        copy.start()
        sides.append(copy)

    fetch.wait()
    xt[...] = x_ref[...].T

    def down(side, zd):
        sbuf, rbuf = ((sbuf_v, rbuf_v), (sbuf_k, rbuf_k))[side]
        return remote(
            sbuf.at[zd], rbuf.at[zd], c_send.at[side, zd], c_recv.at[side, zd], ctx=c - 2
        )

    def step(side, zd):
        own, slots, pslots, sbuf, rbuf, out = (
            (own_v, slot_v, pslot_v, sbuf_v, rbuf_v, gv_ref),
            (own_k, slot_k, pslot_k, sbuf_k, rbuf_k, gk_ref),
        )[side]

        @pl.when(zd <= z)
        def _():
            dest = 2 * zd + y
            value = jnp.zeros(own.shape, F32)
            for owner, held in ((c, slots), (partner, pslots)):
                for j in range(2):
                    gate = jnp.where(picks[owner, j] == dest, 1.0, 0.0).astype(F32)
                    value = value + held[j].astype(F32) * gate
            sbuf[zd] = value.astype(BF16)

            @pl.when(z < lines - 1)
            def _():
                down(side, zd).wait_recv()
                sbuf[zd] = (value + rbuf[zd].astype(F32)).astype(BF16)

            @pl.when(zd < z)
            def _():
                down(side, zd).start()

            @pl.when(zd == z)
            def _():
                out[...] = (sbuf[zd].astype(F32) + own[...]).astype(BF16)

    later = list(range(lines))

    def key_step():
        if later:
            if len(later) == lines:
                sides[1].wait()
            step(1, later.pop(0))

    sides[0].wait()
    for zd in range(lines):
        step(0, zd)
    gv = gv_ref[...]
    rows = x_ref.shape[1] // (n * nf)
    group = x_ref.shape[1] // n
    part = jnp.dot(xt[...], gv, preferred_element_type=F32)
    for cc in range(n):
        for ff in range(nf):
            at = cc * group + ff * rows
            acc[ff, cc] = part[at : at + rows]

    slot = 0
    copies = []
    for stage, bit in enumerate(bits_of(nf)):
        mine = (f // bit) % 2
        low = f % bit
        now = []
        for hi in range(nf // (2 * bit)):
            away = hi * 2 * bit + (1 - mine) * bit + low
            wsend[slot] = acc[away].astype(BF16)
            copy = remote(
                wsend.at[slot], wrecv.at[slot], f_send.at[slot], f_recv.at[slot],
                fsdp=f + bit - 2 * bit * mine,
            )
            copy.start()
            now.append((copy, hi * 2 * bit + mine * bit + low, slot))
            slot += 1
        key_step()
        for copy, keep, at in now:
            copy.wait()
            acc[keep] += wrecv[at].astype(F32)
    for zz in range(lines):
        ysend_buf[zz] = acc[f, 2 * zz + (1 - y)].astype(BF16)
    copy = remote(ysend_buf, yrecv_buf, y_sem.at[0], y_sem.at[1], ctx=partner)
    copy.start()
    key_step()
    copy.wait()
    now = []
    for o in range(1, lines):
        zz = (z + o) % lines
        zsend_buf[o] = (acc[f, 2 * zz + y] + yrecv_buf[zz].astype(F32)).astype(BF16)
        copy = remote(
            zsend_buf.at[o], zrecv_buf.at[o], z_send.at[o], z_recv.at[o], ctx=2 * zz + y
        )
        copy.start()
        now.append(copy)
    while later:
        key_step()
    total = acc[f, c] + yrecv_buf[z].astype(F32)
    for o, copy in enumerate(now):
        copy.wait()
        total = total + zrecv_buf[o + 1].astype(F32)
    gw_ref[...] = total.astype(BF16)

    for zd in range(lines):
        @pl.when(zd < z)
        def _():
            down(0, zd).wait_send()
            down(1, zd).wait_send()


def finish_kernel(gk, gv, gw, gk_out, gv_out, gw_out):
    gk_out[...] = gk[...]
    gv_out[...] = gv[...]
    gw_out[...] = gw[...]


def on_device(inputs, queries, key_vectors, w_value, grad_out, block_picks):
    n, nf = lax.axis_size("ctx"), lax.axis_size("fsdp")
    c = lax.axis_index("ctx")
    lines = n // 2
    x, q, k, g, picks = inputs[0], queries[0], key_vectors[0], grad_out[0], block_picks[0]
    dma = pltpu.SemaphoreType.DMA
    vmem = pl.BlockSpec(memory_space=VM)
    hbm = pl.BlockSpec(memory_space=pltpu.HBM)
    smem = pl.BlockSpec(memory_space=pltpu.SMEM)
    ws = w_value.shape[0]
    kall, vall = pl.pallas_call(
        lambda *refs: gather_kernel(n, nf, *refs),
        out_shape=[jax.ShapeDtypeStruct((n, BLOCK, HEAD), BF16)] * 2,
        in_specs=[hbm] * 3,
        out_specs=[vmem] * 2,
        scratch_shapes=[VM(x.shape, BF16), VM((nf, ws, HEAD), BF16), dma((3,)), dma((nf,)), dma((nf,))] + [dma((n,))] * 6,
        compiler_params=pltpu.CompilerParams(
            collective_id=0, has_side_effects=True, vmem_limit_bytes=58 * 2**20
        ),
        name="gather_kv",
    )(x, k, w_value)

    me = c[None].astype(jnp.int32)
    block = (1, BLOCK, HEAD)
    head = pl.BlockSpec((BLOCK, HEAD), lambda h, me, picks: (0, h))
    fixed2 = pl.BlockSpec((BLOCK, HEAD), lambda h, me, picks: (0, 0))
    pair = pl.BlockSpec((2, BLOCK, HEAD), lambda h, me, picks: (0, 0, 0))
    at = [pl.BlockSpec(block, lambda h, me, picks: (me[0], 0, 0))]
    for j in range(2):
        at.append(pl.BlockSpec(block, lambda h, me, picks, j=j: (picks[me[0], j], 0, 0)))
    dq, own_k, own_v, slot_k, slot_v = pl.pallas_call(
        attend_kernel,
        out_shape=[
            jax.ShapeDtypeStruct((BLOCK, GROUP * HEAD), BF16),
            jax.ShapeDtypeStruct((BLOCK, HEAD), F32),
            jax.ShapeDtypeStruct((BLOCK, HEAD), F32),
            jax.ShapeDtypeStruct((2, BLOCK, HEAD), BF16),
            jax.ShapeDtypeStruct((2, BLOCK, HEAD), BF16),
        ],
        grid_spec=pltpu.PrefetchScalarGridSpec(
            num_scalar_prefetch=2,
            grid=(GROUP,),
            in_specs=[head, head, fixed2, at[1], at[2], at[0], at[1], at[2]],
            out_specs=[head, fixed2, fixed2, pair, pair],
            scratch_shapes=[VM((3, BLOCK, HEAD), F32)] * 2,
        ),
        compiler_params=pltpu.CompilerParams(vmem_limit_bytes=40 * 2**20),
        name="attend",
    )(me, picks, q, g, k, kall, kall, vall, vall, vall)

    rows = x.shape[1] // (n * nf)
    line_buf = VM((lines, BLOCK, HEAD), BF16)
    gk, gv, gw = pl.pallas_call(
        lambda *refs: reduce_kernel(n, nf, *refs),
        out_shape=[
            jax.ShapeDtypeStruct((BLOCK, HEAD), BF16),
            jax.ShapeDtypeStruct((BLOCK, HEAD), BF16),
            jax.ShapeDtypeStruct((rows, HEAD), BF16),
        ],
        in_specs=[smem, hbm] + [vmem] * 4,
        out_specs=[vmem] * 3,
        scratch_shapes=[VM((2, BLOCK, HEAD), BF16)] * 2
        + [line_buf] * 4
        + [
            VM((nf, n, rows, HEAD), F32),
            VM((nf, n, rows, HEAD), BF16),
            VM((nf, n, rows, HEAD), BF16),
        ]
        + [VM((lines, rows, HEAD), BF16)] * 4
        + [VM(x.shape, BF16), VM(x.shape[::-1], BF16), dma((1,))]
        + [
            dma((2,)), dma((2,)), dma((2, lines)), dma((2, lines)), dma((nf,)), dma((nf,)),
            dma((2,)), dma((lines,)), dma((lines,)),
        ],
        compiler_params=pltpu.CompilerParams(
            collective_id=1, has_side_effects=True, vmem_limit_bytes=32 * 2**20
        ),
        name="reduce_grads",
    )(picks, x, own_k, own_v, slot_k, slot_v)
    gk, gv, gw = pl.pallas_call(
        finish_kernel,
        out_shape=[jax.ShapeDtypeStruct(a.shape, BF16) for a in (gk, gv, gw)],
        in_specs=[vmem] * 3,
        out_specs=[vmem] * 3,
        compiler_params=pltpu.CompilerParams(vmem_limit_bytes=4 * 2**20),
        name="finish",
    )(gk, gv, gw)
    return dq[None], gk[None], gv[None], gw


def solution(mesh):
    in_specs = (
        P("fsdp", "ctx", None),
        P("fsdp", "ctx", None),
        P("fsdp", "ctx", None),
        P("fsdp", None),
        P("fsdp", "ctx", None),
        P("fsdp", None, None),
    )
    out_specs = (
        P("fsdp", "ctx", None),
        P("fsdp", "ctx", None),
        P("fsdp", "ctx", None),
        P(("ctx", "fsdp"), None),
    )
    return jax.shard_map(
        on_device, mesh=mesh, in_specs=in_specs, out_specs=out_specs, check_vma=False
    )
```

```python
import math

import jax
import jax.numpy as jnp
from jax import lax
from jax.experimental import pallas as pl
from jax.experimental.pallas import tpu as pltpu
from jax.sharding import PartitionSpec as P

HEAD = 128
GROUP = 4
BLOCK = 512
NEG = -1e30
MESH = pl.DeviceIdType.MESH
F32 = jnp.float32
BF16 = jnp.bfloat16
VM = pltpu.VMEM


def bits_of(count):
    bits, bit = [], 1
    while bit < count:
        bits.append(bit)
        bit *= 2
    return bits


def remote(src, dst, send, recv, **where):
    return pltpu.make_async_remote_copy(
        src_ref=src,
        dst_ref=dst,
        send_sem=send,
        recv_sem=recv,
        device_id=where,
        device_id_type=MESH,
    )


def greet(n, nf):
    c, f = lax.axis_index("ctx"), lax.axis_index("fsdp")
    lines = n // 2
    y, z = c % 2, c // 2
    barrier = pltpu.get_barrier_semaphore()
    count = 0
    for bit in bits_of(nf):
        mine = (f // bit) % 2
        pl.semaphore_signal(
            barrier, inc=1, device_id={"fsdp": f + bit - 2 * bit * mine}, device_id_type=MESH
        )
        count += 1
    pl.semaphore_signal(
        barrier, inc=1, device_id={"ctx": 2 * z + (1 - y)}, device_id_type=MESH
    )
    count += 1
    for o in range(1, lines):
        pl.semaphore_signal(
            barrier, inc=1, device_id={"ctx": 2 * ((z + o) % lines) + y}, device_id_type=MESH
        )
        count += 1
    return lambda: pl.semaphore_wait(barrier, count)


def gather_kernel(
    n, nf, x_hbm, k_hbm, w_hbm, kall, vall, x_ref, wbuf, load, w_send, w_recv,
    kz_send, vz_send, ky_send, vy_send, k_recv, v_recv,
):
    c, f = lax.axis_index("ctx"), lax.axis_index("fsdp")
    lines = n // 2
    y, z = c % 2, c // 2
    partner = 2 * z + (1 - y)
    ws = w_hbm.shape[0]
    loads = [
        pltpu.make_async_copy(w_hbm, wbuf.at[f], load.at[0]),
        pltpu.make_async_copy(k_hbm, kall.at[c], load.at[1]),
        pltpu.make_async_copy(x_hbm, x_ref, load.at[2]),
    ]
    for copy in loads:
        copy.start()
    greet(n, nf)()
    loads[0].wait()
    loads[1].wait()

    def up(buf, b, send, recv):
        return remote(buf.at[b], buf.at[b], send.at[b], recv.at[b], ctx=c + 2)

    def across(buf, b, send, recv):
        return remote(buf.at[b], buf.at[b], send.at[b], recv.at[b], ctx=partner)

    held = [f]
    bits = bits_of(nf)
    slot = 0
    stages = []
    for bit in reversed(bits):
        mine = (f // bit) % 2
        other = bit - 2 * bit * mine
        stages.append((bit, other))

    def w_stage(index, held, slot):
        bit, other = stages[index]
        copies = []
        for g in held:
            copies.append(
                remote(wbuf.at[g], wbuf.at[g], w_send.at[slot], w_recv.at[slot], fsdp=f + other)
            )
            slot += 1
        for copy in copies:
            copy.start()
        return copies, [g + other for g in held], slot

    def forward(buf, b, zsend, ysend, recv, first):
        @pl.when(z < lines - 1)
        def _():
            up(buf, b, zsend, recv).start()

        if first:
            @pl.when(y == 0)
            def _():
                across(buf, b, ysend, recv).start()
        else:
            across(buf, b, ysend, recv).start()

    total = None

    def add(total, g):
        columns = pl.ds(pl.multiple_of(g * ws, ws), ws)
        term = jnp.dot(x_ref[:, columns], wbuf[g], preferred_element_type=F32)
        return term if total is None else total + term

    def relay(buf, s, zsend, ysend, recv):
        b = c - 2 * s

        @pl.when(z - s >= 0)
        def _():
            up(buf, b, zsend, recv).wait_recv()
            forward(buf, b, zsend, ysend, recv, False)

    early = 1
    for index in range(len(stages)):
        copies, came, slot = w_stage(index, held, slot)
        if index == 0:
            forward(kall, c, kz_send, ky_send, k_recv, True)
            loads[2].wait()
            total = add(total, f)
            for s in range(1, 1 + early):
                relay(kall, s, kz_send, ky_send, k_recv)
        for copy in copies:
            copy.wait()
        held = held + came
    for g in held[1:]:
        total = add(total, g)
    vall[c] = total.astype(BF16)
    forward(vall, c, vz_send, vy_send, v_recv, True)

    for s in range(1, lines):
        if s + early < lines:
            relay(kall, s + early, kz_send, ky_send, k_recv)
        relay(vall, s, vz_send, vy_send, v_recv)

    @pl.when(y == 1)
    def _():
        across(kall, partner, ky_send, k_recv).wait_recv()
        across(vall, partner, vy_send, v_recv).wait_recv()

    for s in range(1, lines):
        @pl.when(z - s >= 0)
        def _():
            across(kall, partner - 2 * s, ky_send, k_recv).wait_recv()
            across(vall, partner - 2 * s, vy_send, v_recv).wait_recv()

    for s in range(lines):
        b = c - 2 * s

        @pl.when(z - s >= 0)
        def _():
            @pl.when(z < lines - 1)
            def _():
                up(kall, b, kz_send, k_recv).wait_send()
                up(vall, b, vz_send, v_recv).wait_send()

            def done():
                across(kall, b, ky_send, k_recv).wait_send()
                across(vall, b, vy_send, v_recv).wait_send()

            if s == 0:
                pl.when(y == 0)(done)
            else:
                done()


def reduce_kernel(
    n, nf, picks, x_ref, q_ref, g_ref, kall, vall, dq_ref, gk_ref, gv_ref, gw_ref,
    ksel, vsel, ktr, lows, dk_acc, dv_acc, slot_k, slot_v,
    pslot_k, pslot_v, sbuf_k, sbuf_v, rbuf_k, rbuf_v, acc, wsend, wrecv, ysend_buf, yrecv_buf,
    zsend_buf, zrecv_buf, xt, p_send, p_recv, c_send, c_recv, f_send, f_recv, y_sem, z_send, z_recv,
):
    c, f = lax.axis_index("ctx"), lax.axis_index("fsdp")
    lines = n // 2
    y, z = c % 2, c // 2
    partner = 2 * z + (1 - y)
    entered = greet(n, nf)
    inv_root = 1.0 / math.sqrt(HEAD)
    scale = inv_root / math.log(2.0)
    nt = (((1,), (1,)), ((), ()))
    ksel[0] = kall[c]
    vsel[0] = vall[c]
    for j in range(2):
        ksel[j + 1] = kall[picks[c, j]]
        vsel[j + 1] = vall[picks[c, j]]
    for j in range(3):
        ktr[j] = ksel[j].T
    use = [picks[c, j] != c for j in range(2)]
    dk_acc[...] = jnp.zeros_like(dk_acc)
    dv_acc[...] = jnp.zeros_like(dv_acc)

    def columns(h):
        return pl.ds(pl.multiple_of(h * HEAD, HEAD), HEAD)

    def value_pass(h, carry):
        q, g = q_ref[:, columns(h)], g_ref[:, columns(h)]
        scores, tops = [], []
        for j in range(3):
            s = lax.dot_general(ksel[j], q, nt, preferred_element_type=F32)
            if j == 0:
                u = lax.broadcasted_iota(jnp.int32, s.shape, 0)
                t = lax.broadcasted_iota(jnp.int32, s.shape, 1)
                s = jnp.where(u <= t, s, NEG)
            scores.append(s)
            tops.append(jnp.max(s, axis=0, keepdims=True))
        highest = tops[0]
        for j in range(2):
            highest = jnp.maximum(highest, jnp.where(use[j], tops[j + 1], NEG))
        highest = highest * scale
        shifts = [highest] + [jnp.where(use[j], highest, -NEG) for j in range(2)]
        exps = [jnp.exp2(s * scale - shift) for s, shift in zip(scores, shifts)]
        norm = 1.0 / sum(jnp.sum(e, axis=0, keepdims=True) for e in exps)
        for j in range(3):
            low = (exps[j] * norm).astype(BF16)
            lows[h, j] = low
            dv_acc[j] += jnp.dot(low, g, preferred_element_type=F32)
        return carry

    lax.fori_loop(0, GROUP, value_pass, 0)
    for j in range(2):
        slot_v[j] = dv_acc[j + 1].astype(BF16)
    entered()
    sides = []
    for side, (slots, pslots) in enumerate(((slot_v, pslot_v), (slot_k, pslot_k))):
        sides.append(remote(slots, pslots, p_send.at[side], p_recv.at[side], ctx=partner))
    sides[0].start()

    def down(side, zd):
        sbuf, rbuf = ((sbuf_v, rbuf_v), (sbuf_k, rbuf_k))[side]
        return remote(
            sbuf.at[zd], rbuf.at[zd], c_send.at[side, zd], c_recv.at[side, zd], ctx=c - 2
        )

    def step(side, zd):
        own, slots, pslots, sbuf, rbuf, out = (
            (dv_acc, slot_v, pslot_v, sbuf_v, rbuf_v, gv_ref),
            (dk_acc, slot_k, pslot_k, sbuf_k, rbuf_k, gk_ref),
        )[side]

        @pl.when(zd <= z)
        def _():
            dest = 2 * zd + y
            value = jnp.zeros(own.shape[1:], F32)
            for owner, held in ((c, slots), (partner, pslots)):
                for j in range(2):
                    gate = jnp.where(picks[owner, j] == dest, 1.0, 0.0).astype(F32)
                    value = value + held[j].astype(F32) * gate
            sbuf[zd] = value.astype(BF16)

            @pl.when(z < lines - 1)
            def _():
                down(side, zd).wait_recv()
                sbuf[zd] = (value + rbuf[zd].astype(F32)).astype(BF16)

            @pl.when(zd < z)
            def _():
                down(side, zd).start()

            @pl.when(zd == z)
            def _():
                out[...] = (sbuf[zd].astype(F32) + own[0]).astype(BF16)

    later = list(range(lines))

    def key_step():
        if later:
            if len(later) == lines:
                sides[1].wait()
            step(1, later.pop(0))

    def value_steps():
        sides[0].wait()
        for zd in range(lines):
            step(0, zd)

    def key_pass(h, carry):
        q, g = q_ref[:, columns(h)], g_ref[:, columns(h)]
        dws = [lax.dot_general(vsel[j], g, nt, preferred_element_type=F32) for j in range(3)]
        delta = sum(
            jnp.sum(lows[h, j].astype(F32) * dws[j], axis=0, keepdims=True) for j in range(3)
        )
        dq = jnp.zeros((HEAD, BLOCK), F32)
        for j in range(3):
            ds = (lows[h, j].astype(F32) * (dws[j] - delta)).astype(BF16)
            dk_acc[j] += jnp.dot(ds, q, preferred_element_type=F32)
            dq = dq + jnp.dot(ktr[j], ds, preferred_element_type=F32)
        dq_ref[:, columns(h)] = (dq * inv_root).T.astype(BF16)
        pl.when((h == 1) & (z == lines - 1))(value_steps)
        return carry

    lax.fori_loop(0, GROUP, key_pass, 0)
    dk_acc[...] = dk_acc[...] * inv_root
    for j in range(2):
        slot_k[j] = dk_acc[j + 1].astype(BF16)
    sides[1].start()
    xt[...] = x_ref[...].T
    pl.when(z != lines - 1)(value_steps)
    gv = gv_ref[...]
    rows = x_ref.shape[1] // (n * nf)
    group = x_ref.shape[1] // n
    part = jnp.dot(xt[...], gv, preferred_element_type=F32)
    for cc in range(n):
        for ff in range(nf):
            at = cc * group + ff * rows
            acc[ff, cc] = part[at : at + rows]

    slot = 0
    copies = []
    for stage, bit in enumerate(bits_of(nf)):
        mine = (f // bit) % 2
        low = f % bit
        now = []
        for hi in range(nf // (2 * bit)):
            away = hi * 2 * bit + (1 - mine) * bit + low
            wsend[slot] = acc[away].astype(BF16)
            copy = remote(
                wsend.at[slot], wrecv.at[slot], f_send.at[slot], f_recv.at[slot],
                fsdp=f + bit - 2 * bit * mine,
            )
            copy.start()
            now.append((copy, hi * 2 * bit + mine * bit + low, slot))
            slot += 1
        key_step()
        for copy, keep, at in now:
            copy.wait()
            acc[keep] += wrecv[at].astype(F32)
    for zz in range(lines):
        ysend_buf[zz] = acc[f, 2 * zz + (1 - y)].astype(BF16)
    copy = remote(ysend_buf, yrecv_buf, y_sem.at[0], y_sem.at[1], ctx=partner)
    copy.start()
    key_step()
    copy.wait()
    now = []
    for o in range(1, lines):
        zz = (z + o) % lines
        zsend_buf[o] = (acc[f, 2 * zz + y] + yrecv_buf[zz].astype(F32)).astype(BF16)
        copy = remote(
            zsend_buf.at[o], zrecv_buf.at[o], z_send.at[o], z_recv.at[o], ctx=2 * zz + y
        )
        copy.start()
        now.append(copy)
    while later:
        key_step()
    total = acc[f, c] + yrecv_buf[z].astype(F32)
    for o, copy in enumerate(now):
        copy.wait()
        total = total + zrecv_buf[o + 1].astype(F32)
    gw_ref[...] = total.astype(BF16)

    for zd in range(lines):
        @pl.when(zd < z)
        def _():
            down(0, zd).wait_send()
            down(1, zd).wait_send()


def finish_kernel(*refs):
    for at in range(4):
        refs[4 + at][...] = refs[at][...]


def on_device(inputs, queries, key_vectors, w_value, grad_out, block_picks):
    n, nf = lax.axis_size("ctx"), lax.axis_size("fsdp")
    c = lax.axis_index("ctx")
    lines = n // 2
    x, q, k, g, picks = inputs[0], queries[0], key_vectors[0], grad_out[0], block_picks[0]
    dma = pltpu.SemaphoreType.DMA
    vmem = pl.BlockSpec(memory_space=VM)
    hbm = pl.BlockSpec(memory_space=pltpu.HBM)
    smem = pl.BlockSpec(memory_space=pltpu.SMEM)
    ws = w_value.shape[0]
    kall, vall = pl.pallas_call(
        lambda *refs: gather_kernel(n, nf, *refs),
        out_shape=[jax.ShapeDtypeStruct((n, BLOCK, HEAD), BF16)] * 2,
        in_specs=[hbm] * 3,
        out_specs=[vmem] * 2,
        scratch_shapes=[VM(x.shape, BF16), VM((nf, ws, HEAD), BF16), dma((3,)), dma((nf,)), dma((nf,))] + [dma((n,))] * 6,
        compiler_params=pltpu.CompilerParams(
            collective_id=0, has_side_effects=True, vmem_limit_bytes=58 * 2**20
        ),
        name="gather_kv",
    )(x, k, w_value)

    rows = x.shape[1] // (n * nf)
    line_buf = VM((lines, BLOCK, HEAD), BF16)
    results = pl.pallas_call(
        lambda *refs: reduce_kernel(n, nf, *refs),
        out_shape=[
            jax.ShapeDtypeStruct((BLOCK, GROUP * HEAD), BF16),
            jax.ShapeDtypeStruct((BLOCK, HEAD), BF16),
            jax.ShapeDtypeStruct((BLOCK, HEAD), BF16),
            jax.ShapeDtypeStruct((rows, HEAD), BF16),
        ],
        in_specs=[smem] + [vmem] * 5,
        out_specs=[vmem] * 4,
        scratch_shapes=[VM((3, BLOCK, HEAD), BF16)] * 2
        + [VM((3, HEAD, BLOCK), BF16), VM((GROUP, 3, BLOCK, BLOCK), BF16)]
        + [VM((3, BLOCK, HEAD), F32)] * 2
        + [VM((2, BLOCK, HEAD), BF16)] * 4
        + [line_buf] * 4
        + [
            VM((nf, n, rows, HEAD), F32),
            VM((nf, n, rows, HEAD), BF16),
            VM((nf, n, rows, HEAD), BF16),
        ]
        + [VM((lines, rows, HEAD), BF16)] * 4
        + [VM(x.shape[::-1], BF16)]
        + [
            dma((2,)), dma((2,)), dma((2, lines)), dma((2, lines)), dma((nf,)), dma((nf,)),
            dma((2,)), dma((lines,)), dma((lines,)),
        ],
        compiler_params=pltpu.CompilerParams(
            collective_id=1, has_side_effects=True, vmem_limit_bytes=42 * 2**20
        ),
        name="reduce_grads",
    )(picks, x, q, g, kall, vall)
    dq, gk, gv, gw = pl.pallas_call(
        finish_kernel,
        out_shape=[jax.ShapeDtypeStruct(a.shape, BF16) for a in results],
        in_specs=[vmem] * 4,
        out_specs=[vmem] * 4,
        compiler_params=pltpu.CompilerParams(vmem_limit_bytes=6 * 2**20),
        name="finish",
    )(*results)
    return dq[None], gk[None], gv[None], gw


def solution(mesh):
    in_specs = (
        P("fsdp", "ctx", None),
        P("fsdp", "ctx", None),
        P("fsdp", "ctx", None),
        P("fsdp", None),
        P("fsdp", "ctx", None),
        P("fsdp", None, None),
    )
    out_specs = (
        P("fsdp", "ctx", None),
        P("fsdp", "ctx", None),
        P("fsdp", "ctx", None),
        P(("ctx", "fsdp"), None),
    )
    return jax.shard_map(
        on_device, mesh=mesh, in_specs=in_specs, out_specs=out_specs, check_vma=False
    )
```

```python
import math

import jax
import jax.numpy as jnp
from jax import lax
from jax.experimental import pallas as pl
from jax.experimental.pallas import tpu as pltpu
from jax.sharding import PartitionSpec as P

HEAD = 128
GROUP = 4
BLOCK = 512
NEG = -1e30
MESH = pl.DeviceIdType.MESH
F32 = jnp.float32
BF16 = jnp.bfloat16
VM = pltpu.VMEM


def bits_of(count):
    bits, bit = [], 1
    while bit < count:
        bits.append(bit)
        bit *= 2
    return bits


def remote(src, dst, send, recv, **where):
    return pltpu.make_async_remote_copy(
        src_ref=src,
        dst_ref=dst,
        send_sem=send,
        recv_sem=recv,
        device_id=where,
        device_id_type=MESH,
    )


def greet(n, nf):
    c, f = lax.axis_index("ctx"), lax.axis_index("fsdp")
    lines = n // 2
    y, z = c % 2, c // 2
    barrier = pltpu.get_barrier_semaphore()
    count = 0
    for bit in bits_of(nf):
        mine = (f // bit) % 2
        pl.semaphore_signal(
            barrier, inc=1, device_id={"fsdp": f + bit - 2 * bit * mine}, device_id_type=MESH
        )
        count += 1
    pl.semaphore_signal(
        barrier, inc=1, device_id={"ctx": 2 * z + (1 - y)}, device_id_type=MESH
    )
    count += 1
    for o in range(1, lines):
        pl.semaphore_signal(
            barrier, inc=1, device_id={"ctx": 2 * ((z + o) % lines) + y}, device_id_type=MESH
        )
        count += 1
    return lambda: pl.semaphore_wait(barrier, count)


def gather_kernel(
    n, nf, x_hbm, k_hbm, w_hbm, kall, vall, x_ref, wbuf, load, w_send, w_recv,
    kz_send, vz_send, ky_send, vy_send, k_recv, v_recv,
):
    c, f = lax.axis_index("ctx"), lax.axis_index("fsdp")
    lines = n // 2
    y, z = c % 2, c // 2
    partner = 2 * z + (1 - y)
    ws = w_hbm.shape[0]
    loads = [
        pltpu.make_async_copy(w_hbm, wbuf.at[f], load.at[0]),
        pltpu.make_async_copy(k_hbm, kall.at[c], load.at[1]),
        pltpu.make_async_copy(x_hbm, x_ref, load.at[2]),
    ]
    for copy in loads:
        copy.start()
    greet(n, nf)()
    loads[0].wait()
    loads[1].wait()

    def up(buf, b, send, recv):
        return remote(buf.at[b], buf.at[b], send.at[b], recv.at[b], ctx=c + 2)

    def across(buf, b, send, recv):
        return remote(buf.at[b], buf.at[b], send.at[b], recv.at[b], ctx=partner)

    held = [f]
    bits = bits_of(nf)
    slot = 0
    stages = []
    for bit in reversed(bits):
        mine = (f // bit) % 2
        other = bit - 2 * bit * mine
        stages.append((bit, other))

    def w_stage(index, held, slot):
        bit, other = stages[index]
        copies = []
        for g in held:
            copies.append(
                remote(wbuf.at[g], wbuf.at[g], w_send.at[slot], w_recv.at[slot], fsdp=f + other)
            )
            slot += 1
        for copy in copies:
            copy.start()
        return copies, [g + other for g in held], slot

    def forward(buf, b, zsend, ysend, recv, first):
        @pl.when(z < lines - 1)
        def _():
            up(buf, b, zsend, recv).start()

        if first:
            @pl.when(y == 0)
            def _():
                across(buf, b, ysend, recv).start()
        else:
            across(buf, b, ysend, recv).start()

    total = None

    def add(total, g):
        columns = pl.ds(pl.multiple_of(g * ws, ws), ws)
        term = jnp.dot(x_ref[:, columns], wbuf[g], preferred_element_type=F32)
        return term if total is None else total + term

    def relay(buf, s, zsend, ysend, recv):
        b = c - 2 * s

        @pl.when(z - s >= 0)
        def _():
            up(buf, b, zsend, recv).wait_recv()
            forward(buf, b, zsend, ysend, recv, False)

    early = 1
    for index in range(len(stages)):
        copies, came, slot = w_stage(index, held, slot)
        if index == 0:
            forward(kall, c, kz_send, ky_send, k_recv, True)
            loads[2].wait()
            total = add(total, f)
            for s in range(1, 1 + early):
                relay(kall, s, kz_send, ky_send, k_recv)
        for copy in copies:
            copy.wait()
        held = held + came
    for g in held[1:]:
        total = add(total, g)
    vall[c] = total.astype(BF16)
    forward(vall, c, vz_send, vy_send, v_recv, True)

    for s in range(1, lines):
        if s + early < lines:
            relay(kall, s + early, kz_send, ky_send, k_recv)
        relay(vall, s, vz_send, vy_send, v_recv)

    @pl.when(y == 1)
    def _():
        across(kall, partner, ky_send, k_recv).wait_recv()
        across(vall, partner, vy_send, v_recv).wait_recv()

    for s in range(1, lines):
        @pl.when(z - s >= 0)
        def _():
            across(kall, partner - 2 * s, ky_send, k_recv).wait_recv()
            across(vall, partner - 2 * s, vy_send, v_recv).wait_recv()

    for s in range(lines):
        b = c - 2 * s

        @pl.when(z - s >= 0)
        def _():
            @pl.when(z < lines - 1)
            def _():
                up(kall, b, kz_send, k_recv).wait_send()
                up(vall, b, vz_send, v_recv).wait_send()

            def done():
                across(kall, b, ky_send, k_recv).wait_send()
                across(vall, b, vy_send, v_recv).wait_send()

            if s == 0:
                pl.when(y == 0)(done)
            else:
                done()


def reduce_kernel(
    n, nf, picks, x_hbm, q_hbm, g_hbm, k_hbm, v_hbm, dq_ref, gk_ref, gv_ref, gw_ref,
    x_ref, q_ref, g_ref, kall, vall, load, ksel, vsel, ktr, lows, dk_acc, dv_acc, slot_k, slot_v,
    pslot_k, pslot_v, sbuf_k, sbuf_v, rbuf_k, rbuf_v, acc, wsend, wrecv, ysend_buf, yrecv_buf,
    zsend_buf, zrecv_buf, xt, p_send, p_recv, c_send, c_recv, f_send, f_recv, y_sem, z_send, z_recv,
):
    c, f = lax.axis_index("ctx"), lax.axis_index("fsdp")
    lines = n // 2
    y, z = c % 2, c // 2
    partner = 2 * z + (1 - y)
    loads = [
        pltpu.make_async_copy(source, held, load.at[at])
        for at, (source, held) in enumerate(
            ((k_hbm, kall), (v_hbm, vall), (q_hbm, q_ref), (g_hbm, g_ref), (x_hbm, x_ref))
        )
    ]
    for copy in loads:
        copy.start()
    entered = greet(n, nf)
    inv_root = 1.0 / math.sqrt(HEAD)
    scale = inv_root / math.log(2.0)
    nt = (((1,), (1,)), ((), ()))
    dk_acc[...] = jnp.zeros_like(dk_acc)
    dv_acc[...] = jnp.zeros_like(dv_acc)
    for copy in loads[:4]:
        copy.wait()
    ksel[0] = kall[c]
    vsel[0] = vall[c]
    for j in range(2):
        ksel[j + 1] = kall[picks[c, j]]
        vsel[j + 1] = vall[picks[c, j]]
    for j in range(3):
        ktr[j] = ksel[j].T
    use = [picks[c, j] != c for j in range(2)]

    def columns(h):
        return pl.ds(pl.multiple_of(h * HEAD, HEAD), HEAD)

    def value_pass(h, carry):
        q, g = q_ref[:, columns(h)], g_ref[:, columns(h)]
        scores, tops = [], []
        for j in range(3):
            s = lax.dot_general(ksel[j], q, nt, preferred_element_type=F32)
            if j == 0:
                u = lax.broadcasted_iota(jnp.int32, s.shape, 0)
                t = lax.broadcasted_iota(jnp.int32, s.shape, 1)
                s = jnp.where(u <= t, s, NEG)
            scores.append(s)
            tops.append(jnp.max(s, axis=0, keepdims=True))
        highest = tops[0]
        for j in range(2):
            highest = jnp.maximum(highest, jnp.where(use[j], tops[j + 1], NEG))
        highest = highest * scale
        shifts = [highest] + [jnp.where(use[j], highest, -NEG) for j in range(2)]
        exps = [jnp.exp2(s * scale - shift) for s, shift in zip(scores, shifts)]
        norm = 1.0 / sum(jnp.sum(e, axis=0, keepdims=True) for e in exps)
        for j in range(3):
            low = (exps[j] * norm).astype(BF16)
            lows[h, j] = low
            dv_acc[j] += jnp.dot(low, g, preferred_element_type=F32)
        return carry

    lax.fori_loop(0, GROUP, value_pass, 0)
    for j in range(2):
        slot_v[j] = dv_acc[j + 1].astype(BF16)
    entered()
    sides = []
    for side, (slots, pslots) in enumerate(((slot_v, pslot_v), (slot_k, pslot_k))):
        sides.append(remote(slots, pslots, p_send.at[side], p_recv.at[side], ctx=partner))
    sides[0].start()

    def down(side, zd):
        sbuf, rbuf = ((sbuf_v, rbuf_v), (sbuf_k, rbuf_k))[side]
        return remote(
            sbuf.at[zd], rbuf.at[zd], c_send.at[side, zd], c_recv.at[side, zd], ctx=c - 2
        )

    def step(side, zd):
        own, slots, pslots, sbuf, rbuf, out = (
            (dv_acc, slot_v, pslot_v, sbuf_v, rbuf_v, gv_ref),
            (dk_acc, slot_k, pslot_k, sbuf_k, rbuf_k, gk_ref),
        )[side]

        @pl.when(zd <= z)
        def _():
            dest = 2 * zd + y
            value = jnp.zeros(own.shape[1:], F32)
            for owner, held in ((c, slots), (partner, pslots)):
                for j in range(2):
                    gate = jnp.where(picks[owner, j] == dest, 1.0, 0.0).astype(F32)
                    value = value + held[j].astype(F32) * gate
            sbuf[zd] = value.astype(BF16)

            @pl.when(z < lines - 1)
            def _():
                down(side, zd).wait_recv()
                sbuf[zd] = (value + rbuf[zd].astype(F32)).astype(BF16)

            @pl.when(zd < z)
            def _():
                down(side, zd).start()

            @pl.when(zd == z)
            def _():
                out[...] = (sbuf[zd].astype(F32) + own[0]).astype(BF16)

    later = list(range(lines))

    def key_step():
        if later:
            if len(later) == lines:
                sides[1].wait()
            step(1, later.pop(0))

    def value_steps():
        sides[0].wait()
        for zd in range(lines):
            step(0, zd)

    def key_pass(h, carry):
        q, g = q_ref[:, columns(h)], g_ref[:, columns(h)]
        dws = [lax.dot_general(vsel[j], g, nt, preferred_element_type=F32) for j in range(3)]
        delta = sum(
            jnp.sum(lows[h, j].astype(F32) * dws[j], axis=0, keepdims=True) for j in range(3)
        )
        dq = jnp.zeros((HEAD, BLOCK), F32)
        for j in range(3):
            ds = (lows[h, j].astype(F32) * (dws[j] - delta)).astype(BF16)
            dk_acc[j] += jnp.dot(ds, q, preferred_element_type=F32)
            dq = dq + jnp.dot(ktr[j], ds, preferred_element_type=F32)
        dq_ref[:, columns(h)] = (dq * inv_root).T.astype(BF16)
        pl.when((h == 1) & (z == lines - 1))(value_steps)
        return carry

    lax.fori_loop(0, GROUP, key_pass, 0)
    dk_acc[...] = dk_acc[...] * inv_root
    for j in range(2):
        slot_k[j] = dk_acc[j + 1].astype(BF16)
    sides[1].start()
    loads[4].wait()
    xt[...] = x_ref[...].T
    pl.when(z != lines - 1)(value_steps)
    gv = gv_ref[...]
    rows = x_ref.shape[1] // (n * nf)
    group = x_ref.shape[1] // n
    part = jnp.dot(xt[...], gv, preferred_element_type=F32)
    for cc in range(n):
        for ff in range(nf):
            at = cc * group + ff * rows
            acc[ff, cc] = part[at : at + rows]

    slot = 0
    copies = []
    for stage, bit in enumerate(bits_of(nf)):
        mine = (f // bit) % 2
        low = f % bit
        now = []
        for hi in range(nf // (2 * bit)):
            away = hi * 2 * bit + (1 - mine) * bit + low
            wsend[slot] = acc[away].astype(BF16)
            copy = remote(
                wsend.at[slot], wrecv.at[slot], f_send.at[slot], f_recv.at[slot],
                fsdp=f + bit - 2 * bit * mine,
            )
            copy.start()
            now.append((copy, hi * 2 * bit + mine * bit + low, slot))
            slot += 1
        key_step()
        for copy, keep, at in now:
            copy.wait()
            acc[keep] += wrecv[at].astype(F32)
    for zz in range(lines):
        ysend_buf[zz] = acc[f, 2 * zz + (1 - y)].astype(BF16)
    copy = remote(ysend_buf, yrecv_buf, y_sem.at[0], y_sem.at[1], ctx=partner)
    copy.start()
    key_step()
    copy.wait()
    now = []
    for o in range(1, lines):
        zz = (z + o) % lines
        zsend_buf[o] = (acc[f, 2 * zz + y] + yrecv_buf[zz].astype(F32)).astype(BF16)
        copy = remote(
            zsend_buf.at[o], zrecv_buf.at[o], z_send.at[o], z_recv.at[o], ctx=2 * zz + y
        )
        copy.start()
        now.append(copy)
    while later:
        key_step()
    total = acc[f, c] + yrecv_buf[z].astype(F32)
    for o, copy in enumerate(now):
        copy.wait()
        total = total + zrecv_buf[o + 1].astype(F32)
    gw_ref[...] = total.astype(BF16)

    for zd in range(lines):
        @pl.when(zd < z)
        def _():
            down(0, zd).wait_send()
            down(1, zd).wait_send()


def finish_kernel(*refs):
    for at in range(4):
        refs[4 + at][...] = refs[at][...]


def on_device(inputs, queries, key_vectors, w_value, grad_out, block_picks):
    n, nf = lax.axis_size("ctx"), lax.axis_size("fsdp")
    c = lax.axis_index("ctx")
    lines = n // 2
    x, q, k, g, picks = inputs[0], queries[0], key_vectors[0], grad_out[0], block_picks[0]
    dma = pltpu.SemaphoreType.DMA
    vmem = pl.BlockSpec(memory_space=VM)
    hbm = pl.BlockSpec(memory_space=pltpu.HBM)
    smem = pl.BlockSpec(memory_space=pltpu.SMEM)
    ws = w_value.shape[0]
    kall, vall = pl.pallas_call(
        lambda *refs: gather_kernel(n, nf, *refs),
        out_shape=[jax.ShapeDtypeStruct((n, BLOCK, HEAD), BF16)] * 2,
        in_specs=[hbm] * 3,
        out_specs=[vmem] * 2,
        scratch_shapes=[VM(x.shape, BF16), VM((nf, ws, HEAD), BF16), dma((3,)), dma((nf,)), dma((nf,))] + [dma((n,))] * 6,
        compiler_params=pltpu.CompilerParams(
            collective_id=0, has_side_effects=True, vmem_limit_bytes=58 * 2**20
        ),
        name="gather_kv",
    )(x, k, w_value)

    rows = x.shape[1] // (n * nf)
    line_buf = VM((lines, BLOCK, HEAD), BF16)
    results = pl.pallas_call(
        lambda *refs: reduce_kernel(n, nf, *refs),
        out_shape=[
            jax.ShapeDtypeStruct((BLOCK, GROUP * HEAD), BF16),
            jax.ShapeDtypeStruct((BLOCK, HEAD), BF16),
            jax.ShapeDtypeStruct((BLOCK, HEAD), BF16),
            jax.ShapeDtypeStruct((rows, HEAD), BF16),
        ],
        in_specs=[smem] + [hbm] * 5,
        out_specs=[vmem] * 4,
        scratch_shapes=[VM(a.shape, BF16) for a in (x, q, g, kall, vall)]
        + [dma((5,))]
        + [VM((3, BLOCK, HEAD), BF16)] * 2
        + [VM((3, HEAD, BLOCK), BF16), VM((GROUP, 3, BLOCK, BLOCK), BF16)]
        + [VM((3, BLOCK, HEAD), F32)] * 2
        + [VM((2, BLOCK, HEAD), BF16)] * 4
        + [line_buf] * 4
        + [
            VM((nf, n, rows, HEAD), F32),
            VM((nf, n, rows, HEAD), BF16),
            VM((nf, n, rows, HEAD), BF16),
        ]
        + [VM((lines, rows, HEAD), BF16)] * 4
        + [VM(x.shape[::-1], BF16)]
        + [
            dma((2,)), dma((2,)), dma((2, lines)), dma((2, lines)), dma((nf,)), dma((nf,)),
            dma((2,)), dma((lines,)), dma((lines,)),
        ],
        compiler_params=pltpu.CompilerParams(
            collective_id=1, has_side_effects=True, vmem_limit_bytes=58 * 2**20
        ),
        name="reduce_grads",
    )(picks, x, q, g, kall, vall)
    dq, gk, gv, gw = pl.pallas_call(
        finish_kernel,
        out_shape=[jax.ShapeDtypeStruct(a.shape, BF16) for a in results],
        in_specs=[vmem] * 4,
        out_specs=[vmem] * 4,
        compiler_params=pltpu.CompilerParams(vmem_limit_bytes=60 * 2**20),
        name="finish",
    )(*results)
    return dq[None], gk[None], gv[None], gw


def solution(mesh):
    in_specs = (
        P("fsdp", "ctx", None),
        P("fsdp", "ctx", None),
        P("fsdp", "ctx", None),
        P("fsdp", None),
        P("fsdp", "ctx", None),
        P("fsdp", None, None),
    )
    out_specs = (
        P("fsdp", "ctx", None),
        P("fsdp", "ctx", None),
        P("fsdp", "ctx", None),
        P(("ctx", "fsdp"), None),
    )
    return jax.shard_map(
        on_device, mesh=mesh, in_specs=in_specs, out_specs=out_specs, check_vma=False
    )
```
